256 devices in a mesh: tour: 64 (over x_hi, y, z), rows: 4 (over x_lo, core).
Axes of the slice: x: 4 (x_hi: 2, x_lo: 2; x = x_hi * 2 + x_lo), y: 4, z: 8, core: 2. Of those that a mesh axis runs over, the one named last changes fastest.
Arguments:
- iterate: float32 [16384, 8192], P('rows', 'tour'), may hold values from -32 to 32
- right_vectors: float32 [8192, 8192], P('rows', 'tour'), may hold values from -6 to 6
Outputs:
- rotated_matrix: float32 [16384, 8192], P('rows', 'tour')
- rotated_vectors: float32 [8192, 8192], P('rows', 'tour')
The draws below stay inside these ranges and needn't reach their ends.
All inputs are finite; a program needn't handle non-finite values.
Results may differ from the reference program's by a relative error of at most 0.0003.
Values sent between devices are 32-bit elements; how exact they have to be, the bound alone decides.
A program may use at most 64 MiB of HBM per device.

```python
import jax
import jax.numpy as jnp
from jax import lax

M = 16384
BLOCK = 64
ROUNDS = 6
N = 8192
N_TOUR = 64


def draw_iterate(key, part):
    key = jax.random.fold_in(key, 11)
    row_key, col_key, entry_key, left_key, right_key = jax.random.split(key, 5)
    rank = min(32, M // 2)
    order = jnp.arange(rank, dtype=jnp.float32)
    column_scale = jnp.exp(jax.random.uniform(col_key, (1, N), jnp.float32, jnp.log(0.4), jnp.log(4.0)))
    row_scale = jnp.exp(jax.random.uniform(row_key, (M, 1), jnp.float32, jnp.log(0.7), jnp.log(1.4)))
    left_factor = jax.random.truncated_normal(left_key, -3.0, 3.0, (M, rank), jnp.float32)
    right_factor = jax.random.truncated_normal(right_key, -3.0, 3.0, (N, rank), jnp.float32)
    noise = 0.4 * jax.random.truncated_normal(entry_key, -4.0, 4.0, (M, N), jnp.float32)
    weights = 0.85 ** order
    weights = weights / jnp.sqrt(jnp.sum(weights * weights))
    low_rank = jnp.dot(left_factor * weights[None, :], right_factor.T, precision=lax.Precision.HIGHEST)
    entries = 0.7 * low_rank + noise
    return jnp.clip(entries * row_scale * column_scale, -32.0, 32.0)


def steps_of(key, shape, shards, least, largest):
    level, own = 1.0, jax.random.fold_in(key, 6)
    for dim, parts in shards:
        heights = jnp.exp(jax.random.uniform(jax.random.fold_in(own, dim), (parts,), jnp.float32, least / len(shards), largest / len(shards)))
        level = level * jnp.repeat(heights, shape[dim] // parts).reshape([-1 if axis == dim else 1 for axis in range(len(shape))])
    return level


def scatter_about(own_key, shape, deviation, limit, cuts=(), kind=jnp.bfloat16):
    factor_of = steps_of(own_key, shape, cuts, -0.22, 0.18) if cuts else 1.0
    result = jax.random.normal(own_key, shape, jnp.float32) * deviation * factor_of
    return jnp.minimum(jnp.maximum(result, -limit), limit).astype(kind)


def setup_inputs(seed: int = 0) -> dict:
    keys = jax.random.split(jax.random.key(seed), 3)
    iterate = draw_iterate(jax.random.fold_in(keys[2], 71), 0)
    right_vectors = scatter_about(keys[1], (N, N), 1.0, 6.0, ((0, 4), (1, 64)), jnp.float32)
    return dict(iterate=iterate, right_vectors=right_vectors)


EPSILON = 0.25
HIGHEST = lax.Precision.HIGHEST

def cayley(gram_matrix):
    diag_vals = jnp.diagonal(gram_matrix)
    spread = diag_vals[None, :] - diag_vals[:, None]
    totals = diag_vals[None, :] + diag_vals[:, None]
    skewed = gram_matrix * spread / (spread * spread + EPSILON * totals * totals)
    identity = jnp.eye(gram_matrix.shape[0], dtype=gram_matrix.dtype)
    forward = identity + 0.5 * skewed
    system = identity - 0.25 * jnp.dot(skewed, skewed, precision=HIGHEST)
    factor = jnp.linalg.cholesky(system)
    solved = jax.scipy.linalg.cho_solve((factor, True), forward)
    return jnp.dot(forward, solved, precision=HIGHEST)

def advance(matrix_slots):
    upper_half = matrix_slots[:, :, :BLOCK]
    lower_half = matrix_slots[:, :, BLOCK:]
    pair_count = matrix_slots.shape[0]
    new_upper = jnp.concatenate([upper_half[:1], lower_half[:1], upper_half[1:pair_count - 1]], axis=0)
    new_lower = jnp.concatenate([lower_half[1:], upper_half[pair_count - 1:]], axis=0)
    return jnp.concatenate([new_upper, new_lower], axis=2)

def reference(iterate, right_vectors):
    pair_count = N_TOUR
    matrix_slots = iterate.reshape(M, pair_count, 2 * BLOCK).transpose(1, 0, 2)
    vector_slots = right_vectors.reshape(N, pair_count, 2 * BLOCK).transpose(1, 0, 2)
    for round_index in range(ROUNDS):
        gram_stack = jnp.einsum('smi,smj->sij', matrix_slots, matrix_slots, precision=HIGHEST)
        rotations = jax.vmap(cayley)(gram_stack)
        matrix_slots = jnp.einsum('smi,sij->smj', matrix_slots, rotations, precision=HIGHEST)
        vector_slots = jnp.einsum('smi,sij->smj', vector_slots, rotations, precision=HIGHEST)
        matrix_slots = advance(matrix_slots)
        vector_slots = advance(vector_slots)
    rotated_matrix = matrix_slots.transpose(1, 0, 2).reshape(M, N)
    rotated_vectors = vector_slots.transpose(1, 0, 2).reshape(N, N)
    return (rotated_matrix, rotated_vectors)
```

```python
import functools

import jax
import jax.numpy as jnp
from jax import lax
from jax.experimental import pallas as pl
from jax.experimental.pallas import tpu as pltpu
from jax.sharding import PartitionSpec as P

ROUNDS = 6
EPSILON = 0.25
CHUNK = 512
HALF = 64
WIDE = 128
TOP_EIGENVALUE = 336.0
NEWTON_STEPS = 7
MESH = pl.DeviceIdType.MESH


def split(value):
    high = value.astype(jnp.bfloat16)
    return high, (value - high.astype(jnp.float32)).astype(jnp.bfloat16)


def product(left, right):
    dot = functools.partial(jnp.dot, preferred_element_type=jnp.float32)
    return dot(left[0], right[0]) + (dot(left[0], right[1]) + dot(left[1], right[0]))


def exact(left, right):
    return jnp.dot(
        left, right, precision=lax.Precision.HIGHEST, preferred_element_type=jnp.float32)


def rotation_of(gram):
    down = lax.broadcasted_iota(jnp.int32, (WIDE, WIDE), 0)
    across = lax.broadcasted_iota(jnp.int32, (WIDE, WIDE), 1)
    on_diagonal = down == across
    diagonal = jnp.where(on_diagonal, gram, 0.0)
    along = jnp.sum(diagonal, axis=0, keepdims=True)
    upright = jnp.sum(diagonal, axis=1, keepdims=True)
    spread = along - upright
    totals = along + upright
    half = 0.5 * (gram * spread / (spread * spread + EPSILON * totals * totals))
    identity = jnp.where(on_diagonal, 1.0, 0.0).astype(jnp.float32)
    system = identity - exact(half, half)
    scale = 2.0 / (1.0 + TOP_EIGENVALUE)
    error = (TOP_EIGENVALUE - 1.0) / (TOP_EIGENVALUE + 1.0)
    image = scale * system
    inverse = None
    for step in range(NEWTON_STEPS):
        gain = 2.0 / (2.0 - error * error)
        error = error * error / (2.0 - error * error)
        factor = gain * (2.0 * identity - image)
        factor_split = split(factor)
        if inverse is None:
            inverse = scale * factor
        else:
            inverse = product(split(inverse), factor_split)
        if step < NEWTON_STEPS - 1:
            image = product(split(image), factor_split)
    residual = 2.0 * identity - exact(system, inverse)
    forward = exact(identity + half, inverse)
    return 2.0 * exact(forward, residual) - identity


def kernel(
    matrix_in, vectors_in, matrix_out, vectors_out,
    upper, lower, stage, sums, spun, grams,
    load_sem, store_sem, sent_sem, come_sem, gram_sent, gram_come,
):
    slot = lax.axis_index("tour")
    members = lax.axis_size("tour")
    share = lax.axis_index("rows")
    first = slot == 0
    last = slot == members - 1
    crossing = jnp.logical_or(slot == members // 2 - 1, slot == members // 2)
    peers = (share + 1 - 2 * lax.rem(share, 2), lax.rem(share + 2, 4), 3 - share)
    tall = matrix_in.shape[0] // 2
    flat = vectors_in.shape[0] // 2
    chunks = tall // CHUNK
    every = (tall + flat) // CHUNK
    lane = lax.broadcasted_iota(jnp.int32, (CHUNK, WIDE), 1)
    near = lane < HALF

    def rows(c):
        return pl.ds(pl.multiple_of(c * CHUNK, CHUNK), CHUNK)

    def load(part):
        if part == 0:
            return pltpu.make_async_copy(
                matrix_in, stage.at[pl.ds(0, 2 * tall)], load_sem.at[0])
        return pltpu.make_async_copy(
            vectors_in, stage.at[pl.ds(2 * tall, 2 * flat)], load_sem.at[1])

    load(0).start()
    load(1).start()

    barrier = pltpu.get_barrier_semaphore()
    for peer in peers:
        pl.semaphore_signal(barrier, inc=1, device_id={"rows": peer}, device_id_type=MESH)

    @pl.when(jnp.logical_not(first))
    def _():
        pl.semaphore_signal(barrier, inc=1, device_id={"tour": slot - 1}, device_id_type=MESH)

    @pl.when(jnp.logical_not(last))
    def _():
        pl.semaphore_signal(barrier, inc=1, device_id={"tour": slot + 1}, device_id_type=MESH)

    def rightward(r, c):
        return pltpu.make_async_remote_copy(
            upper.at[r, rows(c)], upper.at[r + 1, rows(c)],
            sent_sem.at[0, r, c], come_sem.at[0, r, c],
            device_id={"tour": slot + 1}, device_id_type=MESH)

    def leftward(r, c):
        return pltpu.make_async_remote_copy(
            lower.at[r, rows(c)], lower.at[r + 1, rows(c)],
            sent_sem.at[1, r, c], come_sem.at[1, r, c],
            device_id={"tour": slot - 1}, device_id_type=MESH)

    def turn_first(r, c):
        return pltpu.make_async_copy(
            lower.at[r, rows(c)], upper.at[r + 1, rows(c)], come_sem.at[0, r, c])

    def turn_last(r, c):
        return pltpu.make_async_copy(
            upper.at[r, rows(c)], lower.at[r + 1, rows(c)], come_sem.at[1, r, c])

    def send(r, c):
        @pl.when(last)
        def _():
            turn_last(r, c).start()

        @pl.when(jnp.logical_not(last))
        def _():
            rightward(r, c).start()

        @pl.when(first)
        def _():
            turn_first(r, c).start()

        @pl.when(jnp.logical_not(first))
        def _():
            leftward(r, c).start()

    def receive(r, c):
        @pl.when(first)
        def _():
            turn_first(r, c).wait()

        @pl.when(jnp.logical_not(first))
        def _():
            rightward(r, c).wait_recv()

        @pl.when(last)
        def _():
            turn_last(r, c).wait()

        @pl.when(jnp.logical_not(last))
        def _():
            leftward(r, c).wait_recv()

    def staged(c):
        start = jnp.where(c < chunks, c * CHUNK, 2 * tall + (c - chunks) * CHUNK)
        skip = jnp.where(c < chunks, tall, flat)
        return (
            pl.ds(pl.multiple_of(start, CHUNK), CHUNK),
            pl.ds(pl.multiple_of(start + skip, CHUNK), CHUNK),
        )

    def pack(c, _):
        one, two = staged(c)
        one, two = stage[one], stage[two]
        upper[0, rows(c)] = jnp.where(near, one, pltpu.roll(two, HALF, 1))
        lower[0, rows(c)] = jnp.where(near, pltpu.roll(one, HALF, 1), two)
        return 0

    def add_gram(r, c):
        block = jnp.concatenate([upper[r, rows(c)], lower[r, rows(c)]], axis=1)
        high, low = split(block)
        dims = (((0,), (0,)), ((), ()))
        sums[:, : 2 * WIDE] += lax.dot_general(high, high, dims, preferred_element_type=jnp.float32)
        sums[:, 2 * WIDE :] += lax.dot_general(high, low, dims, preferred_element_type=jnp.float32)

    near_square = lax.broadcasted_iota(jnp.int32, (HALF, WIDE), 1) < HALF

    def folded(at):
        left = sums[:, at : at + WIDE]
        right = sums[:, at + WIDE : at + 2 * WIDE]
        parts = []
        for start in (0, WIDE):
            one, two = slice(start, start + HALF), slice(start + HALF, start + WIDE)
            parts.append(jnp.where(
                near_square,
                left[one] + pltpu.roll(left[two], HALF, 1),
                pltpu.roll(right[one], HALF, 1) + right[two]))
        return jnp.concatenate(parts, axis=0)

    def swap_gram(r, k):
        return pltpu.make_async_remote_copy(
            grams.at[r, share], grams.at[r, share], gram_sent.at[r, k], gram_come.at[r, k],
            device_id={"rows": peers[k]}, device_id_type=MESH)

    def spread_out(rotation):
        columns = []
        for half in (rotation[:HALF], rotation[HALF:]):
            rolled = pltpu.roll(half, HALF, 1)
            columns.append((
                jnp.concatenate([jnp.where(near_square, half, 0.0), jnp.where(near_square, 0.0, rolled)], axis=0),
                jnp.concatenate([jnp.where(near_square, rolled, 0.0), jnp.where(near_square, 0.0, half)], axis=0)))
        to_upper = jnp.concatenate([columns[0][0], columns[1][0]], axis=0)
        to_lower = jnp.concatenate([columns[0][1], columns[1][1]], axis=0)
        return jnp.concatenate(
            [jnp.where(first, to_lower, to_upper), jnp.where(first, to_upper, to_lower)], axis=1)

    def turn(r, c):
        block = jnp.concatenate([upper[r, rows(c)], lower[r, rows(c)]], axis=1)
        result = product(split(block), (spun[0], spun[1]))
        upper[r, rows(c)] = result[:, :WIDE]
        lower[r, rows(c)] = result[:, WIDE:]

    def gram_step(r):
        def step(c, _):
            @pl.when(r > 0)
            def _():
                receive(r - 1, c)

            add_gram(r, c)
            return 0
        return step

    def matrix_step(r):
        def step(c, _):
            turn(r, c)
            send(r, c)
            return 0
        return step

    def vector_step(r):
        def step(c, _):
            @pl.when(r > 0)
            def _():
                receive(r - 1, c)

            turn(r, c)
            send(r, c)
            return 0
        return step

    load(0).wait()
    lax.fori_loop(0, chunks, pack, 0)

    def one_round(r, _):
        sums[...] = jnp.zeros_like(sums)
        lax.fori_loop(0, chunks, gram_step(r), 0)
        cross = folded(2 * WIDE)
        grams[r, share] = folded(0) + (cross + cross.T)

        @pl.when(r == 0)
        def _():
            @pl.when(jnp.logical_or(first, last))
            def _():
                pl.semaphore_wait(barrier, 4)

            @pl.when(jnp.logical_not(jnp.logical_or(first, last)))
            def _():
                pl.semaphore_wait(barrier, 5)

        for k in range(3):
            swap_gram(r, k).start()

        @pl.when(r == 0)
        def _():
            load(1).wait()
            lax.fori_loop(chunks, every, pack, 0)

        for k in range(3):
            swap_gram(r, k).wait_recv()

        @pl.when(jnp.logical_and(crossing, r > 0))
        def _():
            lax.fori_loop(chunks, every, vector_step(r - 1), 0)

        gram = (grams[r, 0] + grams[r, 1]) + (grams[r, 2] + grams[r, 3])
        spun[0], spun[1] = split(spread_out(rotation_of(gram)))
        lax.fori_loop(0, chunks, matrix_step(r), 0)

        @pl.when(jnp.logical_not(crossing))
        def _():
            lax.fori_loop(chunks, every, vector_step(r), 0)

        return 0

    lax.fori_loop(0, ROUNDS, one_round, 0)

    @pl.when(crossing)
    def _():
        lax.fori_loop(chunks, every, vector_step(ROUNDS - 1), 0)

    def store(c, half):
        piece = staged(c)[half]
        return piece

    def finish(kind, out, offset):
        def step(c, _):
            receive(ROUNDS - 1, c)
            one, two = staged(c)
            high, low = upper[ROUNDS, rows(c)], lower[ROUNDS, rows(c)]
            stage[one] = jnp.where(near, high, pltpu.roll(low, HALF, 1))
            stage[two] = jnp.where(near, pltpu.roll(high, HALF, 1), low)
            for half, piece in enumerate((one, two)):
                base = (c - kind * chunks) * CHUNK + half * offset
                pltpu.make_async_copy(
                    stage.at[piece], out.at[pl.ds(pl.multiple_of(base, CHUNK), CHUNK)],
                    store_sem.at[half, c]).start()
            return 0
        return step

    lax.fori_loop(0, chunks, finish(0, matrix_out, tall), 0)
    lax.fori_loop(chunks, every, finish(1, vectors_out, flat), 0)

    def settle(kind, out, offset):
        def step(c, _):
            for half, piece in enumerate(staged(c)):
                base = (c - kind * chunks) * CHUNK + half * offset
                pltpu.make_async_copy(
                    stage.at[piece], out.at[pl.ds(pl.multiple_of(base, CHUNK), CHUNK)],
                    store_sem.at[half, c]).wait()
            return 0
        return step

    def drain(r, _):
        for k in range(3):
            swap_gram(r, k).wait_send()

        def step(c, _):
            @pl.when(jnp.logical_not(last))
            def _():
                rightward(r, c).wait_send()

            @pl.when(jnp.logical_not(first))
            def _():
                leftward(r, c).wait_send()

            return 0

        lax.fori_loop(0, every, step, 0)
        return 0

    lax.fori_loop(0, ROUNDS, drain, 0)
    lax.fori_loop(0, chunks, settle(0, matrix_out, tall), 0)
    lax.fori_loop(chunks, every, settle(1, vectors_out, flat), 0)


def local(iterate, right_vectors):
    tall, flat = iterate.shape[0] // 2, right_vectors.shape[0] // 2
    every = (tall + flat) // CHUNK
    anywhere = pl.BlockSpec(memory_space=pl.ANY)
    return pl.pallas_call(
        kernel,
        out_shape=(
            jax.ShapeDtypeStruct(iterate.shape, jnp.float32),
            jax.ShapeDtypeStruct(right_vectors.shape, jnp.float32),
        ),
        in_specs=[anywhere, anywhere],
        out_specs=(anywhere, anywhere),
        scratch_shapes=[
            pltpu.VMEM((ROUNDS + 1, tall + flat, WIDE), jnp.float32),
            pltpu.VMEM((ROUNDS + 1, tall + flat, WIDE), jnp.float32),
            pltpu.VMEM((2 * (tall + flat), WIDE), jnp.float32),
            pltpu.VMEM((2 * WIDE, 4 * WIDE), jnp.float32),
            pltpu.VMEM((2, 2 * WIDE, 2 * WIDE), jnp.bfloat16),
            pltpu.VMEM((ROUNDS, 4, WIDE, WIDE), jnp.float32),
            pltpu.SemaphoreType.DMA((2,)),
            pltpu.SemaphoreType.DMA((2, every)),
            pltpu.SemaphoreType.DMA((2, ROUNDS, every)),
            pltpu.SemaphoreType.DMA((2, ROUNDS, every)),
            pltpu.SemaphoreType.DMA((ROUNDS, 3)),
            pltpu.SemaphoreType.DMA((ROUNDS, 3)),
        ],
        compiler_params=pltpu.CompilerParams(
            collective_id=0, has_side_effects=True, vmem_limit_bytes=48 * 2**20),
        cost_estimate=pl.CostEstimate(
            flops=6 * ROUNDS * 2 * 2048 * 256 * 256, bytes_accessed=12 * 2**20, transcendentals=0),
    )(iterate, right_vectors)


def solution(mesh):
    placed = (P("rows", "tour"), P("rows", "tour"))
    return jax.shard_map(
        local, mesh=mesh, in_specs=placed, out_specs=placed, check_vma=False)
```

```python
import functools

import jax
import jax.numpy as jnp
from jax import lax
from jax.experimental import pallas as pl
from jax.experimental.pallas import tpu as pltpu
from jax.sharding import PartitionSpec as P

ROUNDS = 6
EPSILON = 0.25
CHUNK = 512
HALF = 64
WIDE = 128
TOP_EIGENVALUE = 336.0
NEWTON_STEPS = 7
MESH = pl.DeviceIdType.MESH


def split(value):
    high = value.astype(jnp.bfloat16)
    return high, (value - high.astype(jnp.float32)).astype(jnp.bfloat16)


def product(left, right):
    dot = functools.partial(jnp.dot, preferred_element_type=jnp.float32)
    return dot(left[0], right[0]) + (dot(left[0], right[1]) + dot(left[1], right[0]))


def exact(left, right):
    return jnp.dot(
        left, right, precision=lax.Precision.HIGHEST, preferred_element_type=jnp.float32)


def rotation_of(gram):
    down = lax.broadcasted_iota(jnp.int32, (WIDE, WIDE), 0)
    across = lax.broadcasted_iota(jnp.int32, (WIDE, WIDE), 1)
    on_diagonal = down == across
    diagonal = jnp.where(on_diagonal, gram, 0.0)
    along = jnp.sum(diagonal, axis=0, keepdims=True)
    upright = jnp.sum(diagonal, axis=1, keepdims=True)
    spread = along - upright
    totals = along + upright
    half = 0.5 * (gram * spread / (spread * spread + EPSILON * totals * totals))
    identity = jnp.where(on_diagonal, 1.0, 0.0).astype(jnp.float32)
    system = identity - exact(half, half)
    scale = 2.0 / (1.0 + TOP_EIGENVALUE)
    error = (TOP_EIGENVALUE - 1.0) / (TOP_EIGENVALUE + 1.0)
    image = scale * system
    inverse = None
    for step in range(NEWTON_STEPS):
        gain = 2.0 / (2.0 - error * error)
        error = error * error / (2.0 - error * error)
        factor = gain * (2.0 * identity - image)
        factor_split = split(factor)
        if inverse is None:
            inverse = scale * factor
        else:
            inverse = product(split(inverse), factor_split)
        if step < NEWTON_STEPS - 1:
            image = product(split(image), factor_split)
    residual = 2.0 * identity - exact(system, inverse)
    forward = exact(identity + half, inverse)
    return 2.0 * exact(forward, residual) - identity


def kernel(
    matrix_in, vectors_in, matrix_out, vectors_out,
    upper, lower, stage, relay, sums, spun, grams,
    load_sem, store_sem, sent_sem, come_sem, relay_sent, relay_come, gram_sent, gram_come,
):
    slot = lax.axis_index("tour")
    members = lax.axis_size("tour")
    share = lax.axis_index("rows")
    first = slot == 0
    last = slot == members - 1
    ends = jnp.logical_or(first, last)
    before, after = members // 2 - 1, members // 2
    leaves_right = slot == before
    leaves_left = slot == after
    crossing = jnp.logical_or(leaves_right, leaves_left)
    next_door = jnp.logical_not(jnp.logical_or(last, leaves_right))
    next_back = jnp.logical_not(jnp.logical_or(first, leaves_left))
    peers = (share + 1 - 2 * lax.rem(share, 2), lax.rem(share + 2, 4), 3 - share)
    tall = matrix_in.shape[0] // 2
    flat = vectors_in.shape[0] // 2
    chunks = tall // CHUNK
    every = (tall + flat) // CHUNK
    lane = lax.broadcasted_iota(jnp.int32, (CHUNK, WIDE), 1)
    near = lane < HALF

    def rows(c):
        return pl.ds(pl.multiple_of(c * CHUNK, CHUNK), CHUNK)

    def load(part):
        if part == 0:
            return pltpu.make_async_copy(
                matrix_in, stage.at[pl.ds(0, 2 * tall)], load_sem.at[0])
        return pltpu.make_async_copy(
            vectors_in, stage.at[pl.ds(2 * tall, 2 * flat)], load_sem.at[1])

    load(0).start()
    load(1).start()

    barrier = pltpu.get_barrier_semaphore()
    for peer in peers:
        pl.semaphore_signal(barrier, inc=1, device_id={"rows": peer}, device_id_type=MESH)

    def greet(other):
        pl.semaphore_signal(barrier, inc=1, device_id={"tour": other}, device_id_type=MESH)

    @pl.when(next_back)
    def _():
        greet(slot - 1)

    @pl.when(next_door)
    def _():
        greet(slot + 1)

    @pl.when(ends)
    def _():
        greet(before)
        greet(after)

    @pl.when(crossing)
    def _():
        greet(0)
        greet(members - 1)

    def rightward(r, c):
        return pltpu.make_async_remote_copy(
            upper.at[r, rows(c)], upper.at[r + 1, rows(c)],
            sent_sem.at[0, r, c], come_sem.at[0, r, c],
            device_id={"tour": slot + 1}, device_id_type=MESH)

    def leftward(r, c):
        return pltpu.make_async_remote_copy(
            lower.at[r, rows(c)], lower.at[r + 1, rows(c)],
            sent_sem.at[1, r, c], come_sem.at[1, r, c],
            device_id={"tour": slot - 1}, device_id_type=MESH)

    def turn_first(r, c):
        return pltpu.make_async_copy(
            lower.at[r, rows(c)], upper.at[r + 1, rows(c)], come_sem.at[0, r, c])

    def turn_last(r, c):
        return pltpu.make_async_copy(
            upper.at[r, rows(c)], lower.at[r + 1, rows(c)], come_sem.at[1, r, c])

    def detour(r, c, toward):
        by_last = lax.rem(c + toward, 2) == 0
        return pltpu.make_async_remote_copy(
            (lower if toward else upper).at[r, rows(c)], relay.at[r, rows(c)],
            sent_sem.at[toward, r, c], relay_come.at[r, c],
            device_id={"tour": jnp.where(by_last, members - 1, 0)}, device_id_type=MESH)

    def forward(r, c, toward):
        return pltpu.make_async_remote_copy(
            relay.at[r, rows(c)], (lower if toward else upper).at[r + 1, rows(c)],
            relay_sent.at[r, c], come_sem.at[toward, r, c],
            device_id={"tour": before if toward else after}, device_id_type=MESH)

    def forwarded_left(c):
        return lax.rem(c + jnp.where(first, 1, 0), 2) == 1

    def pass_on(r):
        def step(c, _):
            arrival(r, c).wait_recv()

            @pl.when(forwarded_left(c))
            def _():
                forward(r, c, 1).start()

            @pl.when(jnp.logical_not(forwarded_left(c)))
            def _():
                forward(r, c, 0).start()

            return 0
        return step

    def arrival(r, c):
        return pltpu.make_async_remote_copy(
            relay.at[r, rows(c)], relay.at[r, rows(c)], relay_sent.at[r, c], relay_come.at[r, c],
            device_id={"tour": before}, device_id_type=MESH)

    def send(r, c):
        @pl.when(last)
        def _():
            turn_last(r, c).start()

        @pl.when(leaves_right)
        def _():
            detour(r, c, 0).start()

        @pl.when(next_door)
        def _():
            rightward(r, c).start()

        @pl.when(first)
        def _():
            turn_first(r, c).start()

        @pl.when(leaves_left)
        def _():
            detour(r, c, 1).start()

        @pl.when(next_back)
        def _():
            leftward(r, c).start()

    def receive(r, c):
        @pl.when(first)
        def _():
            turn_first(r, c).wait()

        @pl.when(jnp.logical_not(first))
        def _():
            rightward(r, c).wait_recv()

        @pl.when(last)
        def _():
            turn_last(r, c).wait()

        @pl.when(jnp.logical_not(last))
        def _():
            leftward(r, c).wait_recv()

    def staged(c):
        start = jnp.where(c < chunks, c * CHUNK, 2 * tall + (c - chunks) * CHUNK)
        skip = jnp.where(c < chunks, tall, flat)
        return (
            pl.ds(pl.multiple_of(start, CHUNK), CHUNK),
            pl.ds(pl.multiple_of(start + skip, CHUNK), CHUNK),
        )

    def pack(c, _):
        one, two = staged(c)
        one, two = stage[one], stage[two]
        upper[0, rows(c)] = jnp.where(near, one, pltpu.roll(two, HALF, 1))
        lower[0, rows(c)] = jnp.where(near, pltpu.roll(one, HALF, 1), two)
        return 0

    def add_gram(r, c):
        block = jnp.concatenate([upper[r, rows(c)], lower[r, rows(c)]], axis=1)
        high, low = split(block)
        dims = (((0,), (0,)), ((), ()))
        sums[:, : 2 * WIDE] += lax.dot_general(high, high, dims, preferred_element_type=jnp.float32)
        sums[:, 2 * WIDE :] += lax.dot_general(high, low, dims, preferred_element_type=jnp.float32)

    near_square = lax.broadcasted_iota(jnp.int32, (HALF, WIDE), 1) < HALF

    def folded(at):
        left = sums[:, at : at + WIDE]
        right = sums[:, at + WIDE : at + 2 * WIDE]
        parts = []
        for start in (0, WIDE):
            one, two = slice(start, start + HALF), slice(start + HALF, start + WIDE)
            parts.append(jnp.where(
                near_square,
                left[one] + pltpu.roll(left[two], HALF, 1),
                pltpu.roll(right[one], HALF, 1) + right[two]))
        return jnp.concatenate(parts, axis=0)

    def swap_gram(r, k):
        return pltpu.make_async_remote_copy(
            grams.at[r, share], grams.at[r, share], gram_sent.at[r, k], gram_come.at[r, k],
            device_id={"rows": peers[k]}, device_id_type=MESH)

    def spread_out(rotation):
        columns = []
        for half in (rotation[:HALF], rotation[HALF:]):
            rolled = pltpu.roll(half, HALF, 1)
            columns.append((
                jnp.concatenate([jnp.where(near_square, half, 0.0), jnp.where(near_square, 0.0, rolled)], axis=0),
                jnp.concatenate([jnp.where(near_square, rolled, 0.0), jnp.where(near_square, 0.0, half)], axis=0)))
        to_upper = jnp.concatenate([columns[0][0], columns[1][0]], axis=0)
        to_lower = jnp.concatenate([columns[0][1], columns[1][1]], axis=0)
        return jnp.concatenate(
            [jnp.where(first, to_lower, to_upper), jnp.where(first, to_upper, to_lower)], axis=1)

    def turn(r, c):
        block = jnp.concatenate([upper[r, rows(c)], lower[r, rows(c)]], axis=1)
        result = product(split(block), (spun[0], spun[1]))
        upper[r, rows(c)] = result[:, :WIDE]
        lower[r, rows(c)] = result[:, WIDE:]

    def gram_step(r):
        def step(c, _):
            @pl.when(r > 0)
            def _():
                receive(r - 1, c)

            add_gram(r, c)
            return 0
        return step

    def matrix_step(r):
        def step(c, _):
            turn(r, c)
            send(r, c)
            return 0
        return step

    def vector_step(r):
        def step(c, _):
            @pl.when(r > 0)
            def _():
                receive(r - 1, c)

            turn(r, c)
            send(r, c)
            return 0
        return step

    load(0).wait()
    lax.fori_loop(0, chunks, pack, 0)

    def one_round(r, _):
        sums[...] = jnp.zeros_like(sums)
        lax.fori_loop(0, chunks, gram_step(r), 0)
        cross = folded(2 * WIDE)
        grams[r, share] = folded(0) + (cross + cross.T)

        @pl.when(r == 0)
        def _():
            @pl.when(jnp.logical_or(ends, crossing))
            def _():
                pl.semaphore_wait(barrier, 6)

            @pl.when(jnp.logical_not(jnp.logical_or(ends, crossing)))
            def _():
                pl.semaphore_wait(barrier, 5)

        for k in range(3):
            swap_gram(r, k).start()

        @pl.when(r == 0)
        def _():
            load(1).wait()
            lax.fori_loop(chunks, every, pack, 0)

        for k in range(3):
            swap_gram(r, k).wait_recv()
        gram = (grams[r, 0] + grams[r, 1]) + (grams[r, 2] + grams[r, 3])
        spun[0], spun[1] = split(spread_out(rotation_of(gram)))
        lax.fori_loop(0, chunks, matrix_step(r), 0)
        lax.fori_loop(chunks, every, vector_step(r), 0)

        @pl.when(ends)
        def _():
            lax.fori_loop(0, every, pass_on(r), 0)

        return 0

    lax.fori_loop(0, ROUNDS, one_round, 0)

    def finish(kind, out, offset):
        def step(c, _):
            receive(ROUNDS - 1, c)
            one, two = staged(c)
            high, low = upper[ROUNDS, rows(c)], lower[ROUNDS, rows(c)]
            stage[one] = jnp.where(near, high, pltpu.roll(low, HALF, 1))
            stage[two] = jnp.where(near, pltpu.roll(high, HALF, 1), low)
            for half, piece in enumerate((one, two)):
                base = (c - kind * chunks) * CHUNK + half * offset
                pltpu.make_async_copy(
                    stage.at[piece], out.at[pl.ds(pl.multiple_of(base, CHUNK), CHUNK)],
                    store_sem.at[half, c]).start()
            return 0
        return step

    lax.fori_loop(0, chunks, finish(0, matrix_out, tall), 0)
    lax.fori_loop(chunks, every, finish(1, vectors_out, flat), 0)

    def settle(kind, out, offset):
        def step(c, _):
            for half, piece in enumerate(staged(c)):
                base = (c - kind * chunks) * CHUNK + half * offset
                pltpu.make_async_copy(
                    stage.at[piece], out.at[pl.ds(pl.multiple_of(base, CHUNK), CHUNK)],
                    store_sem.at[half, c]).wait()
            return 0
        return step

    def drain(r, _):
        for k in range(3):
            swap_gram(r, k).wait_send()

        def step(c, _):
            @pl.when(next_door)
            def _():
                rightward(r, c).wait_send()

            @pl.when(leaves_right)
            def _():
                detour(r, c, 0).wait_send()

            @pl.when(next_back)
            def _():
                leftward(r, c).wait_send()

            @pl.when(leaves_left)
            def _():
                detour(r, c, 1).wait_send()

            @pl.when(ends)
            def _():
                arrival(r, c).wait_send()

            return 0

        lax.fori_loop(0, every, step, 0)
        return 0

    lax.fori_loop(0, ROUNDS, drain, 0)
    lax.fori_loop(0, chunks, settle(0, matrix_out, tall), 0)
    lax.fori_loop(chunks, every, settle(1, vectors_out, flat), 0)


def local(iterate, right_vectors):
    tall, flat = iterate.shape[0] // 2, right_vectors.shape[0] // 2
    every = (tall + flat) // CHUNK
    anywhere = pl.BlockSpec(memory_space=pl.ANY)
    return pl.pallas_call(
        kernel,
        out_shape=(
            jax.ShapeDtypeStruct(iterate.shape, jnp.float32),
            jax.ShapeDtypeStruct(right_vectors.shape, jnp.float32),
        ),
        in_specs=[anywhere, anywhere],
        out_specs=(anywhere, anywhere),
        scratch_shapes=[
            pltpu.VMEM((ROUNDS + 1, tall + flat, WIDE), jnp.float32),
            pltpu.VMEM((ROUNDS + 1, tall + flat, WIDE), jnp.float32),
            pltpu.VMEM((2 * (tall + flat), WIDE), jnp.float32),
            pltpu.VMEM((ROUNDS, tall + flat, WIDE), jnp.float32),
            pltpu.VMEM((2 * WIDE, 4 * WIDE), jnp.float32),
            pltpu.VMEM((2, 2 * WIDE, 2 * WIDE), jnp.bfloat16),
            pltpu.VMEM((ROUNDS, 4, WIDE, WIDE), jnp.float32),
            pltpu.SemaphoreType.DMA((2,)),
            pltpu.SemaphoreType.DMA((2, every)),
            pltpu.SemaphoreType.DMA((2, ROUNDS, every)),
            pltpu.SemaphoreType.DMA((2, ROUNDS, every)),
            pltpu.SemaphoreType.DMA((ROUNDS, every)),
            pltpu.SemaphoreType.DMA((ROUNDS, every)),
            pltpu.SemaphoreType.DMA((ROUNDS, 3)),
            pltpu.SemaphoreType.DMA((ROUNDS, 3)),
        ],
        compiler_params=pltpu.CompilerParams(
            collective_id=0, has_side_effects=True, vmem_limit_bytes=48 * 2**20),
        cost_estimate=pl.CostEstimate(
            flops=6 * ROUNDS * 2 * 2048 * 256 * 256, bytes_accessed=12 * 2**20, transcendentals=0),
    )(iterate, right_vectors)


def solution(mesh):
    placed = (P("rows", "tour"), P("rows", "tour"))
    return jax.shard_map(
        local, mesh=mesh, in_specs=placed, out_specs=placed, check_vma=False)
```

```python
import functools

import jax
import jax.numpy as jnp
from jax import lax
from jax.experimental import pallas as pl
from jax.experimental.pallas import tpu as pltpu
from jax.sharding import PartitionSpec as P

ROUNDS = 6
EPSILON = 0.25
CHUNK = 512
HALF = 64
WIDE = 128
TOP_EIGENVALUE = 336.0
NEWTON_STEPS = 7
MESH = pl.DeviceIdType.MESH


def split(value):
    high = value.astype(jnp.bfloat16)
    return high, (value - high.astype(jnp.float32)).astype(jnp.bfloat16)


def product(left, right):
    dot = functools.partial(jnp.dot, preferred_element_type=jnp.float32)
    return dot(left[0], right[0]) + (dot(left[0], right[1]) + dot(left[1], right[0]))


def exact(left, right):
    return jnp.dot(
        left, right, precision=lax.Precision.HIGHEST, preferred_element_type=jnp.float32)


def rotation_of(gram):
    down = lax.broadcasted_iota(jnp.int32, (WIDE, WIDE), 0)
    across = lax.broadcasted_iota(jnp.int32, (WIDE, WIDE), 1)
    on_diagonal = down == across
    diagonal = jnp.where(on_diagonal, gram, 0.0)
    along = jnp.sum(diagonal, axis=0, keepdims=True)
    upright = jnp.sum(diagonal, axis=1, keepdims=True)
    spread = along - upright
    totals = along + upright
    half = 0.5 * (gram * spread / (spread * spread + EPSILON * totals * totals))
    identity = jnp.where(on_diagonal, 1.0, 0.0).astype(jnp.float32)
    system = identity - exact(half, half)
    scale = 2.0 / (1.0 + TOP_EIGENVALUE)
    error = (TOP_EIGENVALUE - 1.0) / (TOP_EIGENVALUE + 1.0)
    image = scale * system
    inverse = None
    for step in range(NEWTON_STEPS):
        gain = 2.0 / (2.0 - error * error)
        error = error * error / (2.0 - error * error)
        factor = gain * (2.0 * identity - image)
        factor_split = split(factor)
        if inverse is None:
            inverse = scale * factor
        else:
            inverse = product(split(inverse), factor_split)
        if step < NEWTON_STEPS - 1:
            image = product(split(image), factor_split)
    residual = 2.0 * identity - exact(system, inverse)
    forward = exact(identity + half, inverse)
    return 2.0 * exact(forward, residual) - identity


def kernel(
    matrix_in, vectors_in, matrix_out, vectors_out,
    upper, lower, stage, relay, sums, spun, grams,
    load_sem, store_sem, sent_sem, come_sem, relay_sent, relay_come, gram_sent, gram_come,
):
    slot = lax.axis_index("tour")
    members = lax.axis_size("tour")
    share = lax.axis_index("rows")
    first = slot == 0
    last = slot == members - 1
    ends = jnp.logical_or(first, last)
    before, after = members // 2 - 1, members // 2
    leaves_right = slot == before
    leaves_left = slot == after
    crossing = jnp.logical_or(leaves_right, leaves_left)
    next_door = jnp.logical_not(jnp.logical_or(last, leaves_right))
    next_back = jnp.logical_not(jnp.logical_or(first, leaves_left))
    peers = (share + 1 - 2 * lax.rem(share, 2), lax.rem(share + 2, 4), 3 - share)
    tall = matrix_in.shape[0] // 2
    flat = vectors_in.shape[0] // 2
    chunks = tall // CHUNK
    every = (tall + flat) // CHUNK
    lane = lax.broadcasted_iota(jnp.int32, (CHUNK, WIDE), 1)
    near = lane < HALF

    def rows(c):
        return pl.ds(pl.multiple_of(c * CHUNK, CHUNK), CHUNK)

    def load(part):
        if part == 0:
            return pltpu.make_async_copy(
                matrix_in, stage.at[pl.ds(0, 2 * tall)], load_sem.at[0])
        return pltpu.make_async_copy(
            vectors_in, stage.at[pl.ds(2 * tall, 2 * flat)], load_sem.at[1])

    load(0).start()
    load(1).start()

    barrier = pltpu.get_barrier_semaphore()
    for peer in peers:
        pl.semaphore_signal(barrier, inc=1, device_id={"rows": peer}, device_id_type=MESH)

    def greet(other):
        pl.semaphore_signal(barrier, inc=1, device_id={"tour": other}, device_id_type=MESH)

    @pl.when(next_back)
    def _():
        greet(slot - 1)

    @pl.when(next_door)
    def _():
        greet(slot + 1)

    @pl.when(ends)
    def _():
        greet(before)
        greet(after)

    @pl.when(crossing)
    def _():
        greet(0)
        greet(members - 1)

    def rightward(r, c):
        return pltpu.make_async_remote_copy(
            upper.at[r, rows(c)], upper.at[r + 1, rows(c)],
            sent_sem.at[0, r, c], come_sem.at[0, r, c],
            device_id={"tour": slot + 1}, device_id_type=MESH)

    def leftward(r, c):
        return pltpu.make_async_remote_copy(
            lower.at[r, rows(c)], lower.at[r + 1, rows(c)],
            sent_sem.at[1, r, c], come_sem.at[1, r, c],
            device_id={"tour": slot - 1}, device_id_type=MESH)

    def turn_first(r, c):
        return pltpu.make_async_copy(
            lower.at[r, rows(c)], upper.at[r + 1, rows(c)], come_sem.at[0, r, c])

    def turn_last(r, c):
        return pltpu.make_async_copy(
            upper.at[r, rows(c)], lower.at[r + 1, rows(c)], come_sem.at[1, r, c])

    def detour(r, c, toward):
        by_last = lax.rem(c + toward, 2) == 0
        return pltpu.make_async_remote_copy(
            (lower if toward else upper).at[r, rows(c)], relay.at[r, rows(c)],
            sent_sem.at[toward, r, c], relay_come.at[r, c],
            device_id={"tour": jnp.where(by_last, members - 1, 0)}, device_id_type=MESH)

    def forward(r, c, toward):
        return pltpu.make_async_remote_copy(
            relay.at[r, rows(c)], (lower if toward else upper).at[r + 1, rows(c)],
            relay_sent.at[r, c], come_sem.at[toward, r, c],
            device_id={"tour": before if toward else after}, device_id_type=MESH)

    def forwarded_left(c):
        return lax.rem(c + jnp.where(first, 1, 0), 2) == 1

    def pass_on(r):
        def step(c, _):
            arrival(r, c).wait_recv()

            @pl.when(forwarded_left(c))
            def _():
                forward(r, c, 1).start()

            @pl.when(jnp.logical_not(forwarded_left(c)))
            def _():
                forward(r, c, 0).start()

            return 0
        return step

    def arrival(r, c):
        return pltpu.make_async_remote_copy(
            relay.at[r, rows(c)], relay.at[r, rows(c)], relay_sent.at[r, c], relay_come.at[r, c],
            device_id={"tour": before}, device_id_type=MESH)

    def send(r, c):
        @pl.when(last)
        def _():
            turn_last(r, c).start()

        @pl.when(leaves_right)
        def _():
            detour(r, c, 0).start()

        @pl.when(next_door)
        def _():
            rightward(r, c).start()

        @pl.when(first)
        def _():
            turn_first(r, c).start()

        @pl.when(leaves_left)
        def _():
            detour(r, c, 1).start()

        @pl.when(next_back)
        def _():
            leftward(r, c).start()

    def receive(r, c):
        @pl.when(first)
        def _():
            turn_first(r, c).wait()

        @pl.when(jnp.logical_not(first))
        def _():
            rightward(r, c).wait_recv()

        @pl.when(last)
        def _():
            turn_last(r, c).wait()

        @pl.when(jnp.logical_not(last))
        def _():
            leftward(r, c).wait_recv()

    def staged(c):
        start = jnp.where(c < chunks, c * CHUNK, 2 * tall + (c - chunks) * CHUNK)
        skip = jnp.where(c < chunks, tall, flat)
        return (
            pl.ds(pl.multiple_of(start, CHUNK), CHUNK),
            pl.ds(pl.multiple_of(start + skip, CHUNK), CHUNK),
        )

    def pack(c, _):
        one, two = staged(c)
        one, two = stage[one], stage[two]
        upper[0, rows(c)] = jnp.where(near, one, pltpu.roll(two, HALF, 1))
        lower[0, rows(c)] = jnp.where(near, pltpu.roll(one, HALF, 1), two)
        return 0

    def add_gram(r, c):
        block = jnp.concatenate([upper[r, rows(c)], lower[r, rows(c)]], axis=1)
        high, low = split(block)
        dims = (((0,), (0,)), ((), ()))
        sums[:, : 2 * WIDE] += lax.dot_general(high, high, dims, preferred_element_type=jnp.float32)
        sums[:, 2 * WIDE :] += lax.dot_general(high, low, dims, preferred_element_type=jnp.float32)

    near_square = lax.broadcasted_iota(jnp.int32, (HALF, WIDE), 1) < HALF

    def folded(at):
        left = sums[:, at : at + WIDE]
        right = sums[:, at + WIDE : at + 2 * WIDE]
        parts = []
        for start in (0, WIDE):
            one, two = slice(start, start + HALF), slice(start + HALF, start + WIDE)
            parts.append(jnp.where(
                near_square,
                left[one] + pltpu.roll(left[two], HALF, 1),
                pltpu.roll(right[one], HALF, 1) + right[two]))
        return jnp.concatenate(parts, axis=0)

    near_quarter = near_square[: HALF // 2]

    def packed(gram):
        top, bottom = gram[:HALF], gram[HALF:]
        corner = jnp.where(
            near_quarter, pltpu.roll(top[: HALF // 2], HALF, 1), top[HALF // 2 :])
        return jnp.concatenate([jnp.where(near_square, top, bottom), corner], axis=0)

    def unpacked(pieces):
        ends_of, corner = pieces[:HALF], pieces[HALF:]
        beside = jnp.concatenate([pltpu.roll(corner, HALF, 1), corner], axis=0)
        upper_part = jnp.concatenate(
            [jnp.where(near_square, ends_of, beside), jnp.where(near_square, 0.0, ends_of)], axis=0)
        mirrored = upper_part.T
        return jnp.concatenate(
            [upper_part[:HALF], jnp.where(near_square, mirrored[HALF:], upper_part[HALF:])], axis=0)

    def swap_gram(r, k):
        return pltpu.make_async_remote_copy(
            grams.at[r, share], grams.at[r, share], gram_sent.at[r, k], gram_come.at[r, k],
            device_id={"rows": peers[k]}, device_id_type=MESH)

    def spread_out(rotation):
        columns = []
        for half in (rotation[:HALF], rotation[HALF:]):
            rolled = pltpu.roll(half, HALF, 1)
            columns.append((
                jnp.concatenate([jnp.where(near_square, half, 0.0), jnp.where(near_square, 0.0, rolled)], axis=0),
                jnp.concatenate([jnp.where(near_square, rolled, 0.0), jnp.where(near_square, 0.0, half)], axis=0)))
        to_upper = jnp.concatenate([columns[0][0], columns[1][0]], axis=0)
        to_lower = jnp.concatenate([columns[0][1], columns[1][1]], axis=0)
        return jnp.concatenate(
            [jnp.where(first, to_lower, to_upper), jnp.where(first, to_upper, to_lower)], axis=1)

    def turn(r, c):
        block = jnp.concatenate([upper[r, rows(c)], lower[r, rows(c)]], axis=1)
        result = product(split(block), (spun[0], spun[1]))
        upper[r, rows(c)] = result[:, :WIDE]
        lower[r, rows(c)] = result[:, WIDE:]

    def gram_step(r):
        def step(c, _):
            @pl.when(r > 0)
            def _():
                receive(r - 1, c)

            add_gram(r, c)
            return 0
        return step

    def matrix_step(r):
        def step(c, _):
            turn(r, c)
            send(r, c)
            return 0
        return step

    def vector_step(r):
        def step(c, _):
            @pl.when(r > 0)
            def _():
                receive(r - 1, c)

            turn(r, c)
            send(r, c)
            return 0
        return step

    load(0).wait()
    lax.fori_loop(0, chunks, pack, 0)

    def one_round(r, _):
        sums[...] = jnp.zeros_like(sums)
        lax.fori_loop(0, chunks, gram_step(r), 0)
        cross = folded(2 * WIDE)
        grams[r, share] = packed(folded(0) + (cross + cross.T))

        @pl.when(r == 0)
        def _():
            @pl.when(jnp.logical_or(ends, crossing))
            def _():
                pl.semaphore_wait(barrier, 6)

            @pl.when(jnp.logical_not(jnp.logical_or(ends, crossing)))
            def _():
                pl.semaphore_wait(barrier, 5)

        for k in range(3):
            swap_gram(r, k).start()

        @pl.when(r == 0)
        def _():
            load(1).wait()
            lax.fori_loop(chunks, every, pack, 0)

        for k in range(3):
            swap_gram(r, k).wait_recv()
        gram = unpacked((grams[r, 0] + grams[r, 1]) + (grams[r, 2] + grams[r, 3]))
        spun[0], spun[1] = split(spread_out(rotation_of(gram)))
        lax.fori_loop(0, chunks, matrix_step(r), 0)
        lax.fori_loop(chunks, every, vector_step(r), 0)

        @pl.when(ends)
        def _():
            lax.fori_loop(0, every, pass_on(r), 0)

        return 0

    lax.fori_loop(0, ROUNDS, one_round, 0)

    def finish(kind, out, offset):
        def step(c, _):
            receive(ROUNDS - 1, c)
            one, two = staged(c)
            high, low = upper[ROUNDS, rows(c)], lower[ROUNDS, rows(c)]
            stage[one] = jnp.where(near, high, pltpu.roll(low, HALF, 1))
            stage[two] = jnp.where(near, pltpu.roll(high, HALF, 1), low)
            for half, piece in enumerate((one, two)):
                base = (c - kind * chunks) * CHUNK + half * offset
                pltpu.make_async_copy(
                    stage.at[piece], out.at[pl.ds(pl.multiple_of(base, CHUNK), CHUNK)],
                    store_sem.at[half, c]).start()
            return 0
        return step

    lax.fori_loop(0, chunks, finish(0, matrix_out, tall), 0)
    lax.fori_loop(chunks, every, finish(1, vectors_out, flat), 0)

    def settle(kind, out, offset):
        def step(c, _):
            for half, piece in enumerate(staged(c)):
                base = (c - kind * chunks) * CHUNK + half * offset
                pltpu.make_async_copy(
                    stage.at[piece], out.at[pl.ds(pl.multiple_of(base, CHUNK), CHUNK)],
                    store_sem.at[half, c]).wait()
            return 0
        return step

    def drain(r, _):
        for k in range(3):
            swap_gram(r, k).wait_send()

        def step(c, _):
            @pl.when(next_door)
            def _():
                rightward(r, c).wait_send()

            @pl.when(leaves_right)
            def _():
                detour(r, c, 0).wait_send()

            @pl.when(next_back)
            def _():
                leftward(r, c).wait_send()

            @pl.when(leaves_left)
            def _():
                detour(r, c, 1).wait_send()

            @pl.when(ends)
            def _():
                arrival(r, c).wait_send()

            return 0

        lax.fori_loop(0, every, step, 0)
        return 0

    lax.fori_loop(0, ROUNDS, drain, 0)
    lax.fori_loop(0, chunks, settle(0, matrix_out, tall), 0)
    lax.fori_loop(chunks, every, settle(1, vectors_out, flat), 0)


def local(iterate, right_vectors):
    tall, flat = iterate.shape[0] // 2, right_vectors.shape[0] // 2
    every = (tall + flat) // CHUNK
    anywhere = pl.BlockSpec(memory_space=pl.ANY)
    return pl.pallas_call(
        kernel,
        out_shape=(
            jax.ShapeDtypeStruct(iterate.shape, jnp.float32),
            jax.ShapeDtypeStruct(right_vectors.shape, jnp.float32),
        ),
        in_specs=[anywhere, anywhere],
        out_specs=(anywhere, anywhere),
        scratch_shapes=[
            pltpu.VMEM((ROUNDS + 1, tall + flat, WIDE), jnp.float32),
            pltpu.VMEM((ROUNDS + 1, tall + flat, WIDE), jnp.float32),
            pltpu.VMEM((2 * (tall + flat), WIDE), jnp.float32),
            pltpu.VMEM((ROUNDS, tall + flat, WIDE), jnp.float32),
            pltpu.VMEM((2 * WIDE, 4 * WIDE), jnp.float32),
            pltpu.VMEM((2, 2 * WIDE, 2 * WIDE), jnp.bfloat16),
            pltpu.VMEM((ROUNDS, 4, HALF + HALF // 2, WIDE), jnp.float32),
            pltpu.SemaphoreType.DMA((2,)),
            pltpu.SemaphoreType.DMA((2, every)),
            pltpu.SemaphoreType.DMA((2, ROUNDS, every)),
            pltpu.SemaphoreType.DMA((2, ROUNDS, every)),
            pltpu.SemaphoreType.DMA((ROUNDS, every)),
            pltpu.SemaphoreType.DMA((ROUNDS, every)),
            pltpu.SemaphoreType.DMA((ROUNDS, 3)),
            pltpu.SemaphoreType.DMA((ROUNDS, 3)),
        ],
        compiler_params=pltpu.CompilerParams(
            collective_id=0, has_side_effects=True, vmem_limit_bytes=48 * 2**20),
        cost_estimate=pl.CostEstimate(
            flops=6 * ROUNDS * 2 * 2048 * 256 * 256, bytes_accessed=12 * 2**20, transcendentals=0),
    )(iterate, right_vectors)


def solution(mesh):
    placed = (P("rows", "tour"), P("rows", "tour"))
    return jax.shard_map(
        local, mesh=mesh, in_specs=placed, out_specs=placed, check_vma=False)
```
